32 devices in a mesh: row: 2 (over x), col: 16 (over z, y, core).
Axes of the slice: x: 2, y: 2, z: 4, core: 2. Of those that a mesh axis runs over, the one named last changes fastest.
Arguments:
- adj_tiles: bfloat16 [2, 16, 20, 128, 128], P('row', 'col'), may hold values from -0.1875 to 0.1875
- tile_row: int32 [2, 16, 20], P('row', 'col'), may hold values from 0 to 15, as said below
- tile_col: int32 [2, 16, 20], P('row', 'col'), may hold values from 0 to 1
- tile_count: int32 [2, 16], P('row', 'col'), may hold values from 0 to 20, as said below
- node_feats: bfloat16 [4096, 512], P(('row', 'col')), may hold values from -6 to 6
- pre_act: bfloat16 [4096, 512], P(('col', 'row')), may hold values from -6 to 6
- out_grad: bfloat16 [4096, 512], P(('row', 'col')), may hold values from -0.08984375 to 0.08984375
- second_weight: bfloat16 [512, 512], replicated, may hold values from -0.25 to 0.25
Outputs:
- grad_first: float32 [512, 512], replicated
- grad_second: float32 [512, 512], replicated
The draws below stay inside these ranges and needn't reach their ends.
Inputs may be any that keep to these rules, and one draw needn't show every extreme that they name: Within one block the slots name distinct tile positions (tile_row, tile_col). `tile_count`: blocks whose node columns meet their node rows hold 10 to 20 live slots, one of them exactly 20; every other block holds at most 8.
All inputs are finite; a program needn't handle non-finite values.
Results may differ from the reference program's by a relative error of at most 0.024.
Values may be sent and summed in bfloat16 or wider, within the bound.
No kernel may reach another device: no remote copies, remote signals or barrier semaphores. Data moves between devices by JAX's collectives and lax.ppermute only.
A program may use at most 128 MiB of HBM per device.

```python
import jax
import jax.numpy as jnp
from jax import lax

HIDDEN_SIZE = 512
FEATS = 512
TILE = 128
NODES = 4096
ROW_SPAN = 2048
COL_SPAN = 256
ROW_TILES = 16
COL_TILES = 2
SLOTS = 20
N_ROW = 2
N_COL = 16


def tile_places(key):
    base_key = jax.random.fold_in(key, 11)
    device_keys = jax.random.split(base_key, N_ROW * N_COL)

    def one_device(device_key):
        return jax.random.permutation(device_key, ROW_TILES * COL_TILES)[:SLOTS]
    placed = jax.vmap(one_device)(device_keys)
    return placed.reshape(N_ROW, N_COL, SLOTS).astype(jnp.int32)


def draw_tile_row(key, part):
    return (tile_places(key) // COL_TILES).astype(jnp.int32)


def draw_tile_col(key, part):
    return (tile_places(key) % COL_TILES).astype(jnp.int32)


def draw_tile_count(key, part):
    base_key = jax.random.fold_in(key, 23)
    dense_key, sparse_key, chosen_key = jax.random.split(base_key, 3)
    grid_rows = jnp.arange(N_ROW, dtype=jnp.int32)[:, None]
    grid_cols = jnp.arange(N_COL, dtype=jnp.int32)[None, :]
    near = (grid_cols * COL_SPAN < (grid_rows + 1) * ROW_SPAN) & ((grid_cols + 1) * COL_SPAN > grid_rows * ROW_SPAN)
    dense = jax.random.randint(dense_key, (N_ROW, N_COL), SLOTS // 2, SLOTS + 1)
    sparse = jax.random.randint(sparse_key, (N_ROW, N_COL), 0, min(8, SLOTS) + 1)
    counts = jnp.where(near, dense, sparse)
    chosen_row = jax.random.randint(chosen_key, (), 0, N_ROW)
    chosen_col = chosen_row * ROW_SPAN // COL_SPAN
    counts = jnp.where((grid_rows == chosen_row) & (grid_cols == chosen_col), SLOTS, counts)
    return counts.astype(jnp.int32)


def with_spikes(result, own_key, source, target, parts, factor):
    def block_of(dim):
        return (jnp.arange(result.shape[dim]) // (result.shape[dim] // parts)).reshape((-1,) + (1,) * (result.ndim - 1 - dim))

    one_side = jax.random.permutation(own_key, parts)[block_of(target)]
    far = (block_of(target) + parts // 2) % parts
    return jnp.where((block_of(source) == one_side) | (block_of(source) == far), factor * result, result)


def level_of(own_key, dims, shards, smallest, top_value):
    level, own = 1.0, jax.random.fold_in(own_key, 6)
    for dim, parts in shards:
        heights = jnp.exp(jax.random.uniform(jax.random.fold_in(own, dim), (parts,), jnp.float32, smallest / len(shards), top_value / len(shards)))
        level = level * jnp.repeat(heights, dims[dim] // parts).reshape([-1 if axis == dim else 1 for axis in range(len(dims))])
    return level


def scatter_about(own_key, shape, deviation, most, cuts=(), kind=jnp.bfloat16):
    result = deviation * jax.random.normal(own_key, shape, jnp.float32)
    if cuts:
        result = result * level_of(own_key, shape, cuts, -0.22, 0.18)
    return jnp.clip(result, -most, most).astype(kind)


def bell_draw_with(stream_key, dims, width, most, cuts, heavy, kind=jnp.bfloat16):
    drawn = width * jax.random.normal(stream_key, dims, jnp.float32)
    if cuts:
        drawn = drawn * level_of(stream_key, dims, cuts, -0.22, 0.18)
    return jnp.clip(with_spikes(drawn, jax.random.fold_in(stream_key, 3), *heavy), -most, most).astype(kind)


def setup_inputs(seed: int = 0) -> dict:
    arg_keys = jax.random.split(jax.random.key(seed), 9)
    adj_tiles = scatter_about(arg_keys[0], (N_ROW, N_COL, SLOTS, TILE, TILE), (TILE * ROW_TILES // 2) ** -0.5, 0.1875, ((0, 2), (1, 16)))
    tile_row = draw_tile_row(jax.random.fold_in(arg_keys[8], 71), 0)
    tile_col = draw_tile_col(jax.random.fold_in(arg_keys[8], 71), 0)
    tile_count = draw_tile_count(jax.random.fold_in(arg_keys[8], 71), 0)
    node_feats = bell_draw_with(arg_keys[4], (NODES, FEATS), 1.0, 6.0, ((0, 32),), (0, 1, 32, 2.75))
    pre_act = bell_draw_with(arg_keys[5], (NODES, HIDDEN_SIZE), 1.0, 6.0, ((0, 32),), (0, 1, 32, 2.75))
    out_grad = scatter_about(arg_keys[6], (NODES, HIDDEN_SIZE), 0.015, 0.08984375, ((0, 32),))
    second_weight = scatter_about(arg_keys[7], (HIDDEN_SIZE, HIDDEN_SIZE), HIDDEN_SIZE ** -0.5, 0.25)
    return {"adj_tiles": adj_tiles, "tile_row": tile_row, "tile_col": tile_col, "tile_count": tile_count, "node_feats": node_feats, "pre_act": pre_act, "out_grad": out_grad, "second_weight": second_weight}


def device_terms(local_tiles, in_index, out_index, live_count, panel, out_tiles, transpose):
    tile_size = local_tiles.shape[1]
    panel_width = panel.shape[1]
    blocked = panel.reshape(-1, tile_size, panel_width)
    gathered = blocked[in_index]
    if transpose:
        products = jnp.einsum("bij,biw->bjw", local_tiles.astype(jnp.float32), gathered.astype(jnp.float32))
    else:
        products = jnp.einsum("bij,bjw->biw", local_tiles.astype(jnp.float32), gathered.astype(jnp.float32))
    present = (jnp.arange(local_tiles.shape[0], dtype=jnp.int32) < live_count).astype(jnp.float32)
    select = (out_index[None, :] == jnp.arange(out_tiles, dtype=jnp.int32)[:, None]).astype(jnp.float32)
    select = select * present[None, :]
    summed = jnp.einsum("ob,bjw->ojw", select, products)
    return summed.reshape(out_tiles * tile_size, panel_width)


def spread_sum(adj_tiles, tile_row, tile_col, tile_count, panel, transpose):
    grid_tiles = adj_tiles.reshape(N_ROW * N_COL, SLOTS, TILE, TILE)
    rows_flat = tile_row.reshape(N_ROW * N_COL, SLOTS)
    cols_flat = tile_col.reshape(N_ROW * N_COL, SLOTS)
    counts_flat = tile_count.reshape(N_ROW * N_COL)
    panel_width = panel.shape[1]
    initial = jnp.zeros((NODES, panel_width), jnp.float32)

    def visit_device(device, running):
        device = jnp.asarray(device).astype(jnp.int32)
        grid_row = device // N_COL
        grid_col = device % N_COL
        if transpose:
            source = lax.dynamic_slice_in_dim(panel, (grid_row * ROW_SPAN).astype(jnp.int32), ROW_SPAN, 0)
            contrib = device_terms(grid_tiles[device], rows_flat[device], cols_flat[device], counts_flat[device], source, COL_TILES, True)
            target_start = (grid_col * COL_SPAN).astype(jnp.int32)
            target_len = COL_SPAN
        else:
            source = lax.dynamic_slice_in_dim(panel, (grid_col * COL_SPAN).astype(jnp.int32), COL_SPAN, 0)
            contrib = device_terms(grid_tiles[device], cols_flat[device], rows_flat[device], counts_flat[device], source, ROW_TILES, False)
            target_start = (grid_row * ROW_SPAN).astype(jnp.int32)
            target_len = ROW_SPAN
        current = lax.dynamic_slice_in_dim(running, target_start, target_len, 0)
        return lax.dynamic_update_slice_in_dim(running, current + contrib, target_start, 0)

    return lax.fori_loop(0, N_ROW * N_COL, visit_device, initial)


def reference(adj_tiles, tile_row, tile_col, tile_count, node_feats, pre_act, out_grad, second_weight):
    hidden_act = jnp.maximum(pre_act, 0)
    back_agg = spread_sum(adj_tiles, tile_row, tile_col, tile_count, out_grad, True).astype(jnp.bfloat16)
    grad_second = lax.dot_general(hidden_act, back_agg, (((0,), (0,)), ((), ())), preferred_element_type=jnp.float32)
    hidden_grad = lax.dot_general(back_agg, second_weight, (((1,), (1,)), ((), ())), preferred_element_type=jnp.float32)
    pre_grad = jnp.where(pre_act > 0, hidden_grad, 0.0).astype(jnp.bfloat16)
    fwd_agg = spread_sum(adj_tiles, tile_row, tile_col, tile_count, pre_grad, False).astype(jnp.bfloat16)
    grad_first = lax.dot_general(node_feats, fwd_agg, (((0,), (0,)), ((), ())), preferred_element_type=jnp.float32)
    return grad_first, grad_second
```

```python
import functools

import jax
import jax.numpy as jnp
from jax import lax
from jax.experimental import pallas as pl
from jax.experimental.pallas import tpu as pltpu
from jax.sharding import PartitionSpec as P

BF16 = jnp.bfloat16
F32 = jnp.float32
SMEM = pl.BlockSpec(memory_space=pltpu.SMEM)
VMEM = pl.BlockSpec(memory_space=pltpu.VMEM)


def nbytes(shape, dtype):
    total = jnp.dtype(dtype).itemsize
    for size in shape:
        total *= size
    return total


def local_kernel(body, scalars, operands, outs, flops, spare=0):
    out_shape = [jax.ShapeDtypeStruct(shape, dtype) for shape, dtype in outs]
    moved = sum(nbytes(o.shape, o.dtype) for o in operands) + sum(nbytes(*o) for o in outs)
    return pl.pallas_call(
        body,
        out_shape=out_shape,
        in_specs=[SMEM] * len(scalars) + [VMEM] * len(operands),
        out_specs=[VMEM] * len(outs),
        compiler_params=pltpu.CompilerParams(vmem_limit_bytes=moved + spare + (4 << 20)),
        cost_estimate=pl.CostEstimate(flops=flops, bytes_accessed=moved, transcendentals=0),
    )(*scalars, *operands)


def mm(a, b):
    return lax.dot_general(a, b, (((1,), (0,)), ((), ())), preferred_element_type=F32)


def mm_nt(a, b):
    return lax.dot_general(a, b, (((1,), (1,)), ((), ())), preferred_element_type=F32)


def mm_tn(a, b):
    return lax.dot_general(a, b, (((0,), (0,)), ((), ())), preferred_element_type=F32)


def dense_body(per_place, count, rows, cols, place, tiles, out):
    tile = tiles.shape[1]
    out[...] = jnp.zeros_like(out)

    def put(t, carry):
        row = rows[t]
        spot = ((row // per_place) ^ place[0]) * per_place + row % per_place
        down = pl.ds(pl.multiple_of(cols[t] * tile, tile), tile)
        along = pl.ds(pl.multiple_of(spot * tile, tile), tile)
        out[down, along] = tiles[t].T
        return carry

    lax.fori_loop(0, count[0], put, 0)


def block_product(own, other, chunks):
    length = chunks[0].shape[0]
    top, low = None, None
    for m, chunk in enumerate(chunks):
        x = chunk[...]
        a = mm(own[:, m * length : (m + 1) * length], x)
        b = mm(other[:, m * length : (m + 1) * length], x)
        top = a if m == 0 else top + a
        low = b if m == 0 else low + b
    return top, low


def part_body(own, other, *refs):
    chunks, out = refs[:-1], refs[-1]
    top, low = block_product(own, other, chunks)
    span = own.shape[0]
    out[:span] = top.astype(BF16)
    out[span:] = low.astype(BF16)


def grad_body(pre_own, pre_other, mine, theirs, near, far, out):
    span = pre_own.shape[0]
    for at, pre, turned in ((0, pre_own, span), (span, pre_other, 0)):
        hidden = mm_nt(mine[at : at + span], near[...]) + mm_nt(theirs[turned : turned + span], far[...])
        out[at : at + span] = jnp.where(pre[...] > 0, hidden, 0.0).astype(BF16)


def solution(mesh):
    n_row, n_col = mesh.shape["row"], mesh.shape["col"]
    places = n_col // 2
    far_size = n_col // 4
    group_size = 2 * n_row

    def permute(value, row_mask, col_mask):
        pairs = []
        for r in range(n_row):
            for c in range(n_col):
                pairs.append((r * n_col + c, (r ^ row_mask) * n_col + (c ^ col_mask)))
        return lax.ppermute(value, ("row", "col"), pairs)

    def to_member(value, m):
        return permute(value, m // 2, (m % 2) * 2)

    def gather(chunk):
        lines = [chunk] + [permute(chunk, 0, 4 * m) for m in range(1, far_size)]
        out = []
        for line in lines:
            out += [line, permute(line, 0, 2)]
        return out

    def all_sum(pieces, group):
        running = pieces[0].astype(F32)
        for m in range(1, group_size):
            running = running + to_member(pieces[m], m).astype(F32)
        sent = running.astype(BF16)
        for m in range(1, far_size):
            running = running + permute(sent, 0, 4 * m).astype(F32)
        done = running.astype(BF16)
        return [done] + [to_member(done, m) for m in range(1, group_size)]

    def shards(adj_tiles, tile_row, tile_col, tile_count, node_feats, pre_act, out_grad, second_weight):
        tiles = adj_tiles[0, 0]
        tile = tiles.shape[1]
        depth, feats = out_grad.shape
        hidden = second_weight.shape[0]
        half = feats // 2
        row_index = lax.axis_index("row").astype(jnp.int32)
        col_index = lax.axis_index("col").astype(jnp.int32)
        core = col_index % 2
        place = col_index // 2
        group = row_index * 2 + place % 2
        span = pre_act.shape[0] * n_row
        rows = depth * n_col
        per_place = 2 * depth // tile

        def fold(x):
            keep = lax.dynamic_slice_in_dim(x, core * half, half, 1)
            give = lax.dynamic_slice_in_dim(x, (1 - core) * half, half, 1)
            got = permute(give, 0, 1)
            first = jnp.where(core == 0, keep, got)
            second = jnp.where(core == 0, got, keep)
            return jnp.concatenate([first, second], axis=0)

        cot = gather(fold(out_grad))
        feat = gather(fold(node_feats))

        (own,) = local_kernel(
            functools.partial(dense_body, per_place),
            [tile_count[0], tile_row[0, 0], tile_col[0, 0], place.reshape(1)],
            [tiles],
            [((span, rows), BF16)],
            0,
        )
        other = permute(own, 0, 1)

        pre_lines = [pre_act] + [permute(pre_act, m, 0) for m in range(1, n_row)]
        pre_own = jnp.zeros((n_row,) + pre_act.shape, BF16)
        for m in range(n_row):
            pre_own = lax.dynamic_update_index_in_dim(pre_own, pre_lines[m], row_index ^ m, 0)
        pre_own = pre_own.reshape(span, hidden)
        pre_other = permute(pre_own, 0, 1)

        work = 2 * 2 * span * rows * half
        (part,) = local_kernel(part_body, [], [own, other] + cot, [((2 * span, half), BF16)], work, 3 * 8 * span * half)
        total = part.astype(F32)
        for m in range(1, n_row):
            total = total + permute(part, m, 0).astype(F32)
        back = total.astype(BF16)
        back_far = permute(back, 0, 1)
        near = lax.dynamic_slice_in_dim(second_weight, core * half, half, 1)
        far = lax.dynamic_slice_in_dim(second_weight, (1 - core) * half, half, 1)
        (pre_grad,) = local_kernel(
            grad_body,
            [],
            [pre_own, pre_other, back, back_far, near, far],
            [((2 * span, hidden), BF16)],
            2 * 2 * span * feats * hidden,
            3 * 4 * span * hidden,
        )

        def second_body(member, pre_a, pre_b, part_ref, *outs):
            act_a = jnp.maximum(pre_a[...], 0)
            act_b = jnp.maximum(pre_b[...], 0)
            piece = hidden // group_size
            result = mm_tn(act_a, part_ref[:span]) + mm_tn(act_b, part_ref[span:])
            result = result.astype(BF16)
            for p in range(group_size):
                for m in range(group_size):
                    @pl.when((member[0] ^ m) == p)
                    def _():
                        outs[m][...] = result[p * piece : (p + 1) * piece]

        second_pieces = local_kernel(
            second_body,
            [group.reshape(1)],
            [pre_own, pre_other, part],
            [((hidden // group_size, half), BF16)] * group_size,
            2 * 2 * span * hidden * half,
            3 * 4 * hidden * half + 4 * span * hidden,
        )

        def first_body(member, own_ref, other_ref, grad_ref, *refs):
            chunks, outs = refs[:places], refs[places:]
            top, low = block_product(own_ref, other_ref, chunks)
            piece = half // group_size
            result = mm_tn(top.astype(BF16), grad_ref[:span]) + mm_tn(low.astype(BF16), grad_ref[span:])
            result = result.astype(BF16)
            for p in range(group_size):
                for m in range(group_size):
                    @pl.when((member[0] ^ m) == p)
                    def _():
                        outs[m][...] = result[p * piece : (p + 1) * piece]

        first_pieces = local_kernel(
            first_body,
            [group.reshape(1)],
            [own, other, pre_grad] + feat,
            [((half // group_size, hidden), BF16)] * group_size,
            work + 2 * 2 * span * half * hidden,
            3 * 8 * span * half + 3 * 4 * half * hidden,
        )

        second_sum = jnp.stack(all_sum(second_pieces, group))
        second_far = permute(second_sum, 0, 1)
        first_sum = jnp.stack(all_sum(first_pieces, group))
        first_far = permute(first_sum, 0, 1)

        def place_body(where_ref, a_ref, b_ref, c_ref, d_ref, first_ref, second_ref):
            member, me = where_ref[0], where_ref[1]
            low, high = half // group_size, hidden // group_size
            for side, a, c in ((0, a_ref, c_ref), (1, b_ref, d_ref)):
                core_of = me ^ side
                for m in range(group_size):
                    at = member ^ m
                    first_ref[pl.ds(pl.multiple_of(core_of * half + at * low, low), low), :] = a[m].astype(F32)
                    second_ref[
                        pl.ds(pl.multiple_of(at * high, high), high),
                        pl.ds(pl.multiple_of(core_of * half, half), half),
                    ] = c[m].astype(F32)

        first, second = local_kernel(
            place_body,
            [jnp.stack([group, core])],
            [first_sum, first_far, second_sum, second_far],
            [((feats, hidden), F32), ((hidden, feats), F32)],
            0,
        )
        return first, second

    in_specs = (
        P("row", "col", None, None, None),
        P("row", "col", None),
        P("row", "col", None),
        P("row", "col"),
        P(("row", "col"), None),
        P(("col", "row"), None),
        P(("row", "col"), None),
        P(),
    )
    out_specs = (P(), P())
    return jax.shard_map(shards, mesh=mesh, in_specs=in_specs, out_specs=out_specs, check_vma=False)
```

```python
import functools

import jax
import jax.numpy as jnp
from jax import lax
from jax.experimental import pallas as pl
from jax.experimental.pallas import tpu as pltpu
from jax.sharding import PartitionSpec as P

BF16 = jnp.bfloat16
F32 = jnp.float32
SMEM = pl.BlockSpec(memory_space=pltpu.SMEM)
VMEM = pl.BlockSpec(memory_space=pltpu.VMEM)


def after(value, earlier):
    return lax.optimization_barrier((value, earlier))[0]


def nbytes(shape, dtype):
    total = jnp.dtype(dtype).itemsize
    for size in shape:
        total *= size
    return total


def local_kernel(body, scalars, operands, outs, flops, spare=0):
    out_shape = [jax.ShapeDtypeStruct(shape, dtype) for shape, dtype in outs]
    moved = sum(nbytes(o.shape, o.dtype) for o in operands) + sum(nbytes(*o) for o in outs)
    return pl.pallas_call(
        body,
        out_shape=out_shape,
        in_specs=[SMEM] * len(scalars) + [VMEM] * len(operands),
        out_specs=[VMEM] * len(outs),
        compiler_params=pltpu.CompilerParams(vmem_limit_bytes=moved + spare + (1 << 19)),
        cost_estimate=pl.CostEstimate(flops=flops, bytes_accessed=moved, transcendentals=0),
    )(*scalars, *operands)


def mm(a, b):
    return lax.dot_general(a, b, (((1,), (0,)), ((), ())), preferred_element_type=F32)


def mm_nt(a, b):
    return lax.dot_general(a, b, (((1,), (1,)), ((), ())), preferred_element_type=F32)


def mm_tn(a, b):
    return lax.dot_general(a, b, (((0,), (0,)), ((), ())), preferred_element_type=F32)


def dense_body(per_place, count, rows, cols, place, tiles, out):
    tile = tiles.shape[1]
    out[...] = jnp.zeros_like(out)

    def put(t, carry):
        row = rows[t]
        spot = ((row // per_place) ^ place[0]) * per_place + row % per_place
        down = pl.ds(pl.multiple_of(cols[t] * tile, tile), tile)
        along = pl.ds(pl.multiple_of(spot * tile, tile), tile)
        out[down, along] = tiles[t].T
        return carry

    lax.fori_loop(0, count[0], put, 0)


def block_product(own, other, chunks, places):
    top, low = 0.0, 0.0
    for x, place in zip(chunks, places):
        length = x.shape[0]
        top = top + mm(own[:, place * length : (place + 1) * length], x)
        low = low + mm(other[:, place * length : (place + 1) * length], x)
    return top, low


def grad_body(pre_own, pre_other, mine, theirs, near, far, out):
    span = pre_own.shape[0]
    for at, pre, turned in ((0, pre_own, span), (span, pre_other, 0)):
        hidden = mm_nt(mine[at : at + span], near[...]) + mm_nt(theirs[turned : turned + span], far[...])
        out[at : at + span] = jnp.where(pre[...] > 0, hidden, 0.0).astype(BF16)


def solution(mesh):
    n_row, n_col = mesh.shape["row"], mesh.shape["col"]
    far_size = n_col // 4
    group_size = 2 * n_row

    def permute(value, row_mask, col_mask, name):
        pairs = []
        for r in range(n_row):
            for c in range(n_col):
                pairs.append((r * n_col + c, (r ^ row_mask) * n_col + (c ^ col_mask)))
        with jax.named_scope(name):
            return lax.ppermute(value, ("row", "col"), pairs)

    def to_member(value, m, name):
        return permute(value, m // 2, (m % 2) * 2, f"{name}_{m}")

    def scatter(pieces, name):
        running = pieces[0].astype(F32)
        for m in range(1, group_size):
            running = running + to_member(pieces[m], m, f"{name}_scatter").astype(F32)
        return running

    def along_line(running, name):
        sent = running.astype(BF16)
        for m in range(1, far_size):
            running = running + permute(sent, 0, 4 * m, f"{name}_line_{m}").astype(F32)
        return running.astype(BF16)

    def collect(done, name):
        mine = jnp.stack([done] + [to_member(done, m, f"{name}_gather") for m in range(1, group_size)])
        return mine, permute(mine, 0, 1, f"{name}_core")

    def shards(adj_tiles, tile_row, tile_col, tile_count, node_feats, pre_act, out_grad, second_weight):
        tiles = adj_tiles[0, 0]
        tile = tiles.shape[1]
        depth, feats = out_grad.shape
        hidden = second_weight.shape[0]
        half = feats // 2
        row_index = lax.axis_index("row").astype(jnp.int32)
        col_index = lax.axis_index("col").astype(jnp.int32)
        core = col_index % 2
        place = col_index // 2
        group = row_index * 2 + place % 2
        span = pre_act.shape[0] * n_row
        rows = depth * n_col
        per_place = 2 * depth // tile

        def fill(lines):
            out = jnp.zeros((n_row,) + lines[0].shape, BF16)
            for m in range(n_row):
                out = lax.dynamic_update_index_in_dim(out, lines[m], row_index ^ m, 0)
            return out.reshape(span, hidden)

        both = jnp.stack([out_grad, node_feats])
        keep = lax.dynamic_slice_in_dim(both, core * half, half, 2)
        give = lax.dynamic_slice_in_dim(both, (1 - core) * half, half, 2)
        got = permute(give, 0, 1, "half_core")
        def lay(i):
            return jnp.concatenate(
                [jnp.where(core == 0, keep[i], got[i]), jnp.where(core == 0, got[i], keep[i])], axis=0
            )

        cot_line, feat_line = {0: lay(0)}, {0: lay(1)}
        (own,) = local_kernel(
            functools.partial(dense_body, per_place),
            [tile_count[0], tile_row[0, 0], tile_col[0, 0], place.reshape(1)],
            [after(tiles, give)],
            [((span, rows), BF16)],
            0,
        )
        other = permute(own, 0, 1, "block_core")
        turned = permute(jnp.stack([cot_line[0], feat_line[0]]), 0, 2, "near_0")
        pre_own = fill([pre_act] + [permute(pre_act, m, 0, f"act_row_{m}") for m in range(1, n_row)])
        pre_other = permute(pre_own, 0, 1, "act_core")
        step = far_size // 2
        while step:
            for m in sorted(cot_line):
                cot_line[m + step] = permute(cot_line[m], 0, 4 * step, f"cot_far_{m + step}")
                feat_line[m + step] = permute(
                    after(feat_line[m], cot_line[m + step]), 0, 4 * step, f"feat_far_{m + step}"
                )
            step //= 2
        order = sorted(cot_line)
        held = {1: (turned, pre_own), far_size // 2: other}
        cot_near = []
        for m in order[1:]:
            line = after(cot_line[m], held[m]) if m in held else cot_line[m]
            cot_near.append(permute(line, 0, 2, f"cot_near_{m}"))
        cot = [cot_line[m] for m in order] + [turned] + cot_near
        early, last = order[1:-1], order[-1]
        rest = permute(jnp.stack([feat_line[m] for m in early]), 0, 2, "feat_near_early")
        feat = [feat_line[m] for m in order] + [turned, rest]
        feat.append(permute(feat_line[last], 0, 2, "feat_near_last"))
        cot = after(cot, pre_other)
        far_at = [2 * m for m in order]
        near_at = [2 * m + 1 for m in order]

        work = 2 * 2 * span * rows * half
        def part_body(own_ref, other_ref, *refs):
            blocks, out = refs[:-1], refs[-1]
            chunks = [x[0] if len(x.shape) == 3 else x[...] for x in blocks]
            top, low = block_product(own_ref, other_ref, chunks, far_at + near_at)
            out[:span] = top.astype(BF16)
            out[span:] = low.astype(BF16)

        (part,) = local_kernel(part_body, [], after([own, other] + cot, pre_other), [((2 * span, half), BF16)], work, 4 * 4 * span * half)
        total = part.astype(F32)
        for m in range(1, n_row):
            got = permute(part, m, 0, f"part_row_{m}")
            total = total + got.astype(F32)
        back = after(total.astype(BF16), feat)
        back_far = permute(back, 0, 1, "back_core")
        weight_near = lax.dynamic_slice_in_dim(second_weight, core * half, half, 1)
        weight_far = lax.dynamic_slice_in_dim(second_weight, (1 - core) * half, half, 1)
        (pre_grad,) = local_kernel(
            grad_body,
            [],
            [pre_own, pre_other, back, back_far, weight_near, weight_far],
            [((2 * span, hidden), BF16)],
            2 * 2 * span * feats * hidden,
            3 * 4 * span * hidden,
        )

        def second_body(member, pre_a, pre_b, part_ref, *outs):
            act_a = jnp.maximum(pre_a[...], 0)
            act_b = jnp.maximum(pre_b[...], 0)
            piece = hidden // group_size
            result = mm_tn(act_a, part_ref[:span]) + mm_tn(act_b, part_ref[span:])
            result = result.astype(BF16)
            for p in range(group_size):
                for m in range(group_size):
                    @pl.when((member[0] ^ m) == p)
                    def _():
                        outs[m][...] = result[p * piece : (p + 1) * piece]

        second_pieces = local_kernel(
            second_body,
            [group.reshape(1)],
            [pre_own, pre_other, part],
            [((hidden // group_size, half), BF16)] * group_size,
            2 * 2 * span * hidden * half,
            3 * 4 * hidden * half + 4 * span * hidden,
        )

        def first_body(member, own_ref, other_ref, grad_ref, *refs):
            blocks, outs = refs[: len(feat)], refs[len(feat) :]
            chunks = [x[...] for x in blocks[:far_size]] + [blocks[far_size][1]]
            chunks += [blocks[far_size + 1][i] for i in range(len(early))] + [blocks[far_size + 2][...]]
            top, low = block_product(own_ref, other_ref, chunks, far_at + near_at)
            piece = half // group_size
            result = mm_tn(top.astype(BF16), grad_ref[:span]) + mm_tn(low.astype(BF16), grad_ref[span:])
            result = result.astype(BF16)
            for p in range(group_size):
                for m in range(group_size):
                    @pl.when((member[0] ^ m) == p)
                    def _():
                        outs[m][...] = result[p * piece : (p + 1) * piece]

        first_pieces = local_kernel(
            first_body,
            [group.reshape(1)],
            [own, other, pre_grad] + feat,
            [((half // group_size, hidden), BF16)] * group_size,
            work + 2 * 2 * span * half * hidden,
            4 * 4 * span * half + 3 * 4 * half * hidden,
        )

        low, high = half // group_size, hidden // group_size

        def place_second(where_ref, a_ref, b_ref, out):
            for side, pieces in ((0, a_ref), (1, b_ref)):
                across = pl.ds(pl.multiple_of((where_ref[1] ^ side) * half, half), half)
                for m in range(group_size):
                    down = pl.ds(pl.multiple_of((where_ref[0] ^ m) * high, high), high)
                    out[down, across] = pieces[m].astype(F32)

        def place_first(where_ref, a_ref, b_ref, out):
            for side, pieces in ((0, a_ref), (1, b_ref)):
                top = (where_ref[1] ^ side) * half
                for m in range(group_size):
                    down = pl.ds(pl.multiple_of(top + (where_ref[0] ^ m) * low, low), low)
                    out[down, :] = pieces[m].astype(F32)

        where = jnp.stack([group, core])
        second_run = scatter(second_pieces, "second")
        first_pieces = after(first_pieces, second_run)
        second_done = along_line(second_run, "second")
        first_run = scatter(first_pieces, "first")
        (second,) = local_kernel(
            place_second, [where], list(collect(second_done, "second")), [((hidden, feats), F32)], 0
        )
        first_done = along_line(first_run, "first")
        (first,) = local_kernel(
            place_first, [where], list(collect(first_done, "first")), [((feats, hidden), F32)], 0
        )
        return first, second

    in_specs = (
        P("row", "col", None, None, None),
        P("row", "col", None),
        P("row", "col", None),
        P("row", "col"),
        P(("row", "col"), None),
        P(("col", "row"), None),
        P(("row", "col"), None),
        P(),
    )
    out_specs = (P(), P())
    return jax.shard_map(shards, mesh=mesh, in_specs=in_specs, out_specs=out_specs, check_vma=False)
```

```python
import functools

import jax
import jax.numpy as jnp
from jax import lax
from jax.experimental import pallas as pl
from jax.experimental.pallas import tpu as pltpu
from jax.sharding import PartitionSpec as P

BF16 = jnp.bfloat16
F32 = jnp.float32
SMEM = pl.BlockSpec(memory_space=pltpu.SMEM)
VMEM = pl.BlockSpec(memory_space=pltpu.VMEM)


def after(value, earlier):
    return lax.optimization_barrier((value, earlier))[0]


def nbytes(shape, dtype):
    total = jnp.dtype(dtype).itemsize
    for size in shape:
        total *= size
    return total


def local_kernel(body, scalars, operands, outs, flops, spare=0):
    out_shape = [jax.ShapeDtypeStruct(shape, dtype) for shape, dtype in outs]
    moved = sum(nbytes(o.shape, o.dtype) for o in operands) + sum(nbytes(*o) for o in outs)
    return pl.pallas_call(
        body,
        out_shape=out_shape,
        in_specs=[SMEM] * len(scalars) + [VMEM] * len(operands),
        out_specs=[VMEM] * len(outs),
        compiler_params=pltpu.CompilerParams(vmem_limit_bytes=moved + spare + (1 << 19)),
        cost_estimate=pl.CostEstimate(flops=flops, bytes_accessed=moved, transcendentals=0),
    )(*scalars, *operands)


def mm(a, b):
    return lax.dot_general(a, b, (((1,), (0,)), ((), ())), preferred_element_type=F32)


def mm_nt(a, b):
    return lax.dot_general(a, b, (((1,), (1,)), ((), ())), preferred_element_type=F32)


def mm_tn(a, b):
    return lax.dot_general(a, b, (((0,), (0,)), ((), ())), preferred_element_type=F32)


def dense_body(per_place, place, count, rows, cols, tiles, keep, give):
    tile = tiles.shape[1]
    keep[...] = jnp.zeros_like(keep)
    give[...] = jnp.zeros_like(give)

    def put(t, carry):
        row = rows[t]
        other = (row // per_place) ^ place[0]
        spot = (other // 2) * per_place + row % per_place
        down = pl.ds(pl.multiple_of(cols[t] * tile, tile), tile)
        along = pl.ds(pl.multiple_of(spot * tile, tile), tile)
        block = tiles[t].T

        @pl.when(other % 2 == 0)
        def _():
            keep[down, along] = block

        @pl.when(other % 2 == 1)
        def _():
            give[down, along] = block

        return carry

    lax.fori_loop(0, count[0], put, 0)


def product_body(far_size, row, *refs):
    blocks, chunks, outs = refs[:4], refs[4 : 4 + far_size], refs[4 + far_size :]
    deep = outs[0].shape[0] // 2
    length = chunks[0].shape[0]
    for m, out in enumerate(outs):
        at = pl.ds(pl.multiple_of((row[0] ^ (m // 2)) * deep, deep), deep)
        for side in range(2):
            block = blocks[2 * (m % 2) + side]
            total = 0.0
            for j, chunk in enumerate(chunks):
                total = total + mm(block[at, j * length : (j + 1) * length], chunk[...])
            out[side * deep : (side + 1) * deep] = total.astype(BF16)


def grad_body(pre_own, pre_other, mine, theirs, near, far, out):
    deep = pre_own.shape[0]
    for at, pre, turned in ((0, pre_own, deep), (deep, pre_other, 0)):
        hidden = mm_nt(mine[at : at + deep], near[...]) + mm_nt(theirs[turned : turned + deep], far[...])
        out[at : at + deep] = jnp.where(pre[...] > 0, hidden, 0.0).astype(BF16)


def solution(mesh):
    n_row, n_col = mesh.shape["row"], mesh.shape["col"]
    far_size = n_col // 4
    group_size = 2 * n_row

    def permute(value, row_mask, col_mask, name):
        pairs = []
        for r in range(n_row):
            for c in range(n_col):
                pairs.append((r * n_col + c, (r ^ row_mask) * n_col + (c ^ col_mask)))
        with jax.named_scope(name):
            return lax.ppermute(value, ("row", "col"), pairs)

    def to_member(value, m, name):
        return permute(value, m // 2, (m % 2) * 2, f"{name}_{m}")

    def scatter(pieces, name):
        running = pieces[0].astype(F32)
        for m in range(1, group_size):
            running = running + to_member(pieces[m], m, f"{name}_scatter").astype(F32)
        return running

    def along_line(running, name):
        sent = running.astype(BF16)
        for m in range(1, far_size):
            running = running + permute(sent, 0, 4 * m, f"{name}_line_{m}").astype(F32)
        return running.astype(BF16)

    def collect(done, name):
        mine = jnp.stack([done] + [to_member(done, m, f"{name}_gather") for m in range(1, group_size)])
        return mine, permute(mine, 0, 1, f"{name}_core")

    def shards(adj_tiles, tile_row, tile_col, tile_count, node_feats, pre_act, out_grad, second_weight):
        tiles = adj_tiles[0, 0]
        tile = tiles.shape[1]
        depth, feats = out_grad.shape
        hidden = second_weight.shape[0]
        half = feats // 2
        row_index = lax.axis_index("row").astype(jnp.int32)
        col_index = lax.axis_index("col").astype(jnp.int32)
        core = col_index % 2
        place = col_index // 2
        group = row_index * 2 + place % 2
        span = pre_act.shape[0] * n_row
        rows = depth * n_col
        per_place = 2 * depth // tile

        both = jnp.stack([out_grad, node_feats])
        keep = lax.dynamic_slice_in_dim(both, core * half, half, 2)
        give = lax.dynamic_slice_in_dim(both, (1 - core) * half, half, 2)
        got = permute(give, 0, 1, "half_core")
        def lay(i):
            return jnp.concatenate(
                [jnp.where(core == 0, keep[i], got[i]), jnp.where(core == 0, got[i], keep[i])], axis=0
            )

        cot_line, feat_line = {0: lay(0)}, {0: lay(1)}
        keep_a, give_a = local_kernel(
            functools.partial(dense_body, per_place),
            [place.reshape(1), tile_count[0], tile_row[0, 0], tile_col[0, 0]],
            [after(tiles, give)],
            [((span, rows // 2), BF16)] * 2,
            0,
        )
        near_a = permute(give_a, 0, 2, "block_near")
        pre_other = permute(after(pre_act, keep_a), 0, 1, "act_core")
        step = far_size // 2
        while step:
            for m in sorted(cot_line):
                cot_line[m + step] = permute(cot_line[m], 0, 4 * step, f"cot_far_{m + step}")
                feat_line[m + step] = permute(
                    after(feat_line[m], cot_line[m + step]), 0, 4 * step, f"feat_far_{m + step}"
                )
            step //= 2
        order = sorted(cot_line)
        late = after(near_a, [cot_line[m] for m in order] + [feat_line[m] for m in order[:-1]])
        blocks = [keep_a, permute(keep_a, 0, 1, "keep_core"), near_a, permute(late, 0, 1, "near_core")]
        deep = pre_act.shape[0]
        work = 2 * 2 * span * rows * half

        def group_sum(lines, name):
            pieces = local_kernel(
                functools.partial(product_body, far_size),
                [row_index.reshape(1)],
                blocks + [lines[m] for m in order],
                [((2 * deep, half), BF16)] * group_size,
                work,
                8 * 4 * deep * half,
            )
            return scatter(pieces, name).astype(BF16)

        back = group_sum(cot_line, "cot")
        back_far = permute(back, 0, 1, "back_core")
        weight_near = lax.dynamic_slice_in_dim(second_weight, core * half, half, 1)
        weight_far = lax.dynamic_slice_in_dim(second_weight, (1 - core) * half, half, 1)
        (pre_grad,) = local_kernel(
            grad_body,
            [],
            [pre_act, pre_other, back, back_far, weight_near, weight_far],
            [((2 * deep, hidden), BF16)],
            2 * 2 * deep * feats * hidden,
            4 * 4 * deep * hidden,
        )
        feat = group_sum(feat_line, "feat")

        def cut(result, member, outs):
            piece = result.shape[0] // group_size
            for p in range(group_size):
                for m in range(group_size):
                    @pl.when((member[0] ^ m) == p)
                    def _():
                        outs[m][...] = result[p * piece : (p + 1) * piece]

        def second_body(member, pre_a, pre_b, back_ref, *outs):
            result = mm_tn(jnp.maximum(pre_a[...], 0), back_ref[:deep])
            result = result + mm_tn(jnp.maximum(pre_b[...], 0), back_ref[deep:])
            cut(result.astype(BF16), member, outs)

        second_pieces = local_kernel(
            second_body,
            [group.reshape(1)],
            [pre_act, pre_other, back],
            [((hidden // group_size, half), BF16)] * group_size,
            2 * 2 * deep * hidden * half,
            4 * 4 * hidden * half + 4 * deep * hidden,
        )

        def first_body(member, feat_ref, grad_ref, *outs):
            cut(mm_tn(feat_ref[...], grad_ref[...]).astype(BF16), member, outs)

        first_pieces = local_kernel(
            first_body,
            [group.reshape(1)],
            [feat, pre_grad],
            [((half // group_size, hidden), BF16)] * group_size,
            2 * 2 * deep * half * hidden,
            4 * 4 * half * hidden,
        )

        low, high = half // group_size, hidden // group_size

        def place_second(where_ref, a_ref, b_ref, out):
            for side, pieces in ((0, a_ref), (1, b_ref)):
                across = pl.ds(pl.multiple_of((where_ref[1] ^ side) * half, half), half)
                for m in range(group_size):
                    down = pl.ds(pl.multiple_of((where_ref[0] ^ m) * high, high), high)
                    out[down, across] = pieces[m].astype(F32)

        def place_first(where_ref, a_ref, b_ref, out):
            for side, pieces in ((0, a_ref), (1, b_ref)):
                top = (where_ref[1] ^ side) * half
                for m in range(group_size):
                    down = pl.ds(pl.multiple_of(top + (where_ref[0] ^ m) * low, low), low)
                    out[down, :] = pieces[m].astype(F32)

        where = jnp.stack([group, core])
        second_run = scatter(second_pieces, "second")
        second_done = along_line(second_run, "second")
        first_run = scatter(first_pieces, "first")
        (second,) = local_kernel(
            place_second, [where], list(collect(second_done, "second")), [((hidden, feats), F32)], 0
        )
        first_done = along_line(first_run, "first")
        (first,) = local_kernel(
            place_first, [where], list(collect(first_done, "first")), [((feats, hidden), F32)], 0
        )
        return first, second

    in_specs = (
        P("row", "col", None, None, None),
        P("row", "col", None),
        P("row", "col", None),
        P("row", "col"),
        P(("row", "col"), None),
        P(("col", "row"), None),
        P(("row", "col"), None),
        P(),
    )
    out_specs = (P(), P())
    return jax.shard_map(shards, mesh=mesh, in_specs=in_specs, out_specs=out_specs, check_vma=False)
```

```python
import functools

import jax
import jax.numpy as jnp
from jax import lax
from jax.experimental import pallas as pl
from jax.experimental.pallas import tpu as pltpu
from jax.sharding import PartitionSpec as P

BF16 = jnp.bfloat16
F32 = jnp.float32
SMEM = pl.BlockSpec(memory_space=pltpu.SMEM)
VMEM = pl.BlockSpec(memory_space=pltpu.VMEM)


def after(value, earlier):
    return lax.optimization_barrier((value, earlier))[0]


def nbytes(shape, dtype):
    total = jnp.dtype(dtype).itemsize
    for size in shape:
        total *= size
    return total


def local_kernel(body, scalars, operands, outs, flops, spare=0):
    out_shape = [jax.ShapeDtypeStruct(shape, dtype) for shape, dtype in outs]
    moved = sum(nbytes(o.shape, o.dtype) for o in operands) + sum(nbytes(*o) for o in outs)
    return pl.pallas_call(
        body,
        out_shape=out_shape,
        in_specs=[SMEM] * len(scalars) + [VMEM] * len(operands),
        out_specs=[VMEM] * len(outs),
        compiler_params=pltpu.CompilerParams(vmem_limit_bytes=moved + spare + (1 << 19)),
        cost_estimate=pl.CostEstimate(flops=flops, bytes_accessed=moved, transcendentals=0),
    )(*scalars, *operands)


def mm(a, b):
    return lax.dot_general(a, b, (((1,), (0,)), ((), ())), preferred_element_type=F32)


def mm_nt(a, b):
    return lax.dot_general(a, b, (((1,), (1,)), ((), ())), preferred_element_type=F32)


def mm_tn(a, b):
    return lax.dot_general(a, b, (((0,), (0,)), ((), ())), preferred_element_type=F32)


def dense_body(per_place, place, count, rows, cols, tiles, keep, give_low, give_high):
    tile = tiles.shape[1]
    for out in (keep, give_low, give_high):
        out[...] = jnp.zeros_like(out)
    cut = give_low.shape[1] // tile
    live = count[0, 0]
    batch = 4 if tiles.shape[0] % 4 == 0 else 1

    def put(n, carry):
        turned = [tiles[n * batch + i].T for i in range(batch)]
        for i in range(batch):
            t = n * batch + i
            row = rows[0, 0, t]
            other = (row // per_place) ^ place[0]
            spot = (other // 2) * per_place + row % per_place
            down = pl.ds(pl.multiple_of(cols[0, 0, t] * tile, tile), tile)

            @pl.when((t < live) & (other % 2 == 0))
            def _():
                keep[down, pl.ds(pl.multiple_of(spot * tile, tile), tile)] = turned[i]

            @pl.when((t < live) & (other % 2 == 1) & (spot < cut))
            def _():
                give_low[down, pl.ds(pl.multiple_of(spot * tile, tile), tile)] = turned[i]

            @pl.when((t < live) & (other % 2 == 1) & (spot >= cut))
            def _():
                give_high[down, pl.ds(pl.multiple_of((spot - cut) * tile, tile), tile)] = turned[i]

        return carry

    lax.fori_loop(0, (live + batch - 1) // batch, put, 0)


def product_body(far_size, row, *refs):
    blocks, chunks, outs = refs[:6], refs[6 : 6 + far_size], refs[6 + far_size :]
    deep = outs[0].shape[0] // 2
    length = chunks[0].shape[0]
    for m, out in enumerate(outs):
        at = pl.ds(pl.multiple_of((row[0] ^ (m // 2)) * deep, deep), deep)
        for side in range(2):
            total = 0.0
            for j, chunk in enumerate(chunks):
                if m % 2 == 0:
                    block, n = blocks[side], j
                else:
                    block, n = blocks[2 + 2 * side + j // (far_size // 2)], j % (far_size // 2)
                total = total + mm(block[at, n * length : (n + 1) * length], chunk[...])
            out[side * deep : (side + 1) * deep] = total.astype(BF16)


def grad_body(pre_own, pre_other, mine, theirs, near, far, out):
    deep = pre_own.shape[0]
    for at, pre, turned in ((0, pre_own, deep), (deep, pre_other, 0)):
        hidden = mm_nt(mine[at : at + deep], near[...]) + mm_nt(theirs[turned : turned + deep], far[...])
        out[at : at + deep] = jnp.where(pre[...] > 0, hidden, 0.0).astype(BF16)


def solution(mesh):
    n_row, n_col = mesh.shape["row"], mesh.shape["col"]
    far_size = n_col // 4
    group_size = 2 * n_row

    def permute(value, row_mask, col_mask, name):
        pairs = []
        for r in range(n_row):
            for c in range(n_col):
                pairs.append((r * n_col + c, (r ^ row_mask) * n_col + (c ^ col_mask)))
        with jax.named_scope(name):
            return lax.ppermute(value, ("row", "col"), pairs)

    def to_member(value, m, name):
        return permute(value, m // 2, (m % 2) * 2, f"{name}_{m}")

    def scatter(pieces, name):
        running = pieces[0].astype(F32)
        for m in range(1, group_size):
            running = running + to_member(pieces[m], m, f"{name}_scatter").astype(F32)
        return running

    def along_line(running, name):
        sent = running.astype(BF16)
        for m in range(1, far_size):
            running = running + permute(sent, 0, 4 * m, f"{name}_line_{m}").astype(F32)
        return running.astype(BF16)

    def collect(done, name):
        mine = jnp.stack([done] + [to_member(done, m, f"{name}_gather") for m in range(1, group_size)])
        return mine, permute(mine, 0, 1, f"{name}_core")

    def shards(adj_tiles, tile_row, tile_col, tile_count, node_feats, pre_act, out_grad, second_weight):
        tiles = adj_tiles[0, 0]
        tile = tiles.shape[1]
        depth, feats = out_grad.shape
        hidden = second_weight.shape[0]
        half = feats // 2
        row_index = lax.axis_index("row").astype(jnp.int32)
        col_index = lax.axis_index("col").astype(jnp.int32)
        core = col_index % 2
        place = col_index // 2
        group = row_index * 2 + place % 2
        span = pre_act.shape[0] * n_row
        rows = depth * n_col
        per_place = 2 * depth // tile

        keep_a, *give_a = local_kernel(
            functools.partial(dense_body, per_place),
            [place.reshape(1), tile_count, tile_row, tile_col],
            [tiles],
            [((span, rows // 2), BF16)] + [((span, rows // 4), BF16)] * 2,
            0,
        )
        both = jnp.stack(after([out_grad, node_feats], keep_a))
        keep = lax.dynamic_slice_in_dim(both, core * half, half, 2)
        give = lax.dynamic_slice_in_dim(both, (1 - core) * half, half, 2)
        got = permute(give, 0, 1, "half_core")
        def lay(i):
            return jnp.concatenate(
                [jnp.where(core == 0, keep[i], got[i]), jnp.where(core == 0, got[i], keep[i])], axis=0
            )

        cot_line, feat_line = {0: lay(0)}, {0: lay(1)}
        near_a = [permute(x, 0, 2, f"block_near_{n}") for n, x in enumerate(give_a)]
        pre_other = permute(after(pre_act, keep_a), 0, 1, "act_core")
        step = far_size // 2
        while step:
            for m in sorted(cot_line):
                cot_line[m + step] = permute(cot_line[m], 0, 4 * step, f"cot_far_{m + step}")
                feat_line[m + step] = permute(
                    after(feat_line[m], cot_line[m + step]), 0, 4 * step, f"feat_far_{m + step}"
                )
            step //= 2
        order = sorted(cot_line)
        late = [after(near_a[0], cot_line[far_size // 2]), after(near_a[1], [cot_line[m] for m in order] + [feat_line[m] for m in order[:-1]])]
        blocks = [keep_a, permute(keep_a, 0, 1, "keep_core")] + near_a
        blocks += [permute(x, 0, 1, f"near_core_{n}") for n, x in enumerate(late)]
        deep = pre_act.shape[0]
        work = 2 * 2 * span * rows * half

        def group_sum(lines, name):
            pieces = local_kernel(
                functools.partial(product_body, far_size),
                [row_index.reshape(1)],
                blocks + [lines[m] for m in order],
                [((2 * deep, half), BF16)] * group_size,
                work,
                8 * 4 * deep * half,
            )
            return scatter(pieces, name).astype(BF16)

        back = group_sum(cot_line, "cot")
        back_far = permute(back, 0, 1, "back_core")
        weight_near = lax.dynamic_slice_in_dim(second_weight, core * half, half, 1)
        weight_far = lax.dynamic_slice_in_dim(second_weight, (1 - core) * half, half, 1)
        (pre_grad,) = local_kernel(
            grad_body,
            [],
            [pre_act, pre_other, back, back_far, weight_near, weight_far],
            [((2 * deep, hidden), BF16)],
            2 * 2 * deep * feats * hidden,
            4 * 4 * deep * hidden,
        )
        feat = group_sum(feat_line, "feat")

        def cut(result, member, outs):
            piece = result.shape[0] // group_size
            for p in range(group_size):
                for m in range(group_size):
                    @pl.when((member[0] ^ m) == p)
                    def _():
                        outs[m][...] = result[p * piece : (p + 1) * piece]

        def second_body(member, pre_a, pre_b, back_ref, *outs):
            result = mm_tn(jnp.maximum(pre_a[...], 0), back_ref[:deep])
            result = result + mm_tn(jnp.maximum(pre_b[...], 0), back_ref[deep:])
            cut(result.astype(BF16), member, outs)

        second_pieces = local_kernel(
            second_body,
            [group.reshape(1)],
            [pre_act, pre_other, back],
            [((hidden // group_size, half), BF16)] * group_size,
            2 * 2 * deep * hidden * half,
            4 * 4 * hidden * half + 4 * deep * hidden,
        )

        def first_body(member, feat_ref, grad_ref, *outs):
            cut(mm_tn(feat_ref[...], grad_ref[...]).astype(BF16), member, outs)

        first_pieces = local_kernel(
            first_body,
            [group.reshape(1)],
            [feat, pre_grad],
            [((half // group_size, hidden), BF16)] * group_size,
            2 * 2 * deep * half * hidden,
            4 * 4 * half * hidden,
        )

        low, high = half // group_size, hidden // group_size

        def place(spot, shape, mine, theirs):
            piece = mine.shape[1:]

            def body(where_ref, a_ref, b_ref, out, wide, sems):
                copies = []
                for side, pieces in ((0, a_ref), (1, b_ref)):
                    for m in range(group_size):
                        n = side * group_size + m
                        wide[n] = pieces[m].astype(F32)
                        target = out.at[spot(where_ref[0] ^ m, where_ref[1] ^ side)]
                        copies.append(pltpu.make_async_copy(wide.at[n], target, sems.at[n]))
                        copies[-1].start()
                for copy in copies:
                    copy.wait()

            size = 4 * shape[0] * shape[1]
            return pl.pallas_call(
                body,
                out_shape=jax.ShapeDtypeStruct(shape, F32),
                in_specs=[SMEM, VMEM, VMEM],
                out_specs=pl.BlockSpec(memory_space=pl.ANY),
                scratch_shapes=[
                    pltpu.VMEM((2 * group_size,) + piece, F32),
                    pltpu.SemaphoreType.DMA((2 * group_size,)),
                ],
                compiler_params=pltpu.CompilerParams(vmem_limit_bytes=2 * size + (1 << 19)),
                cost_estimate=pl.CostEstimate(flops=0, bytes_accessed=2 * size, transcendentals=0),
            )(where, mine, theirs)

        def second_spot(member, side):
            down = pl.ds(pl.multiple_of(member * high, high), high)
            return down, pl.ds(pl.multiple_of(side * half, half), half)

        def first_spot(member, side):
            return pl.ds(pl.multiple_of(side * half + member * low, low), low), slice(None)

        where = jnp.stack([group, core])
        second_run = scatter(second_pieces, "second")
        second_done = along_line(second_run, "second")
        first_run = scatter(first_pieces, "first")
        second = place(second_spot, (hidden, feats), *collect(second_done, "second"))
        first_done = along_line(first_run, "first")
        first = place(first_spot, (feats, hidden), *collect(first_done, "first"))
        return first, second

    in_specs = (
        P("row", "col", None, None, None),
        P("row", "col", None),
        P("row", "col", None),
        P("row", "col"),
        P(("row", "col"), None),
        P(("col", "row"), None),
        P(("row", "col"), None),
        P(),
    )
    out_specs = (P(), P())
    return jax.shard_map(shards, mesh=mesh, in_specs=in_specs, out_specs=out_specs, check_vma=False)
```

```python
import functools

import jax
import jax.numpy as jnp
from jax import lax
from jax.experimental import pallas as pl
from jax.experimental.pallas import tpu as pltpu
from jax.sharding import PartitionSpec as P

BF16 = jnp.bfloat16
F32 = jnp.float32
SMEM = pl.BlockSpec(memory_space=pltpu.SMEM)
VMEM = pl.BlockSpec(memory_space=pltpu.VMEM)


def after(value, earlier):
    return lax.optimization_barrier((value, earlier))[0]


def nbytes(shape, dtype):
    total = jnp.dtype(dtype).itemsize
    for size in shape:
        total *= size
    return total


def local_kernel(body, scalars, operands, outs, flops, spare=0):
    out_shape = [jax.ShapeDtypeStruct(shape, dtype) for shape, dtype in outs]
    moved = sum(nbytes(o.shape, o.dtype) for o in operands) + sum(nbytes(*o) for o in outs)
    return pl.pallas_call(
        body,
        out_shape=out_shape,
        in_specs=[SMEM] * len(scalars) + [VMEM] * len(operands),
        out_specs=[VMEM] * len(outs),
        compiler_params=pltpu.CompilerParams(vmem_limit_bytes=moved + spare + (1 << 19)),
        cost_estimate=pl.CostEstimate(flops=flops, bytes_accessed=moved, transcendentals=0),
    )(*scalars, *operands)


def mm(a, b):
    return lax.dot_general(a, b, (((1,), (0,)), ((), ())), preferred_element_type=F32)


def mm_nt(a, b):
    return lax.dot_general(a, b, (((1,), (1,)), ((), ())), preferred_element_type=F32)


def mm_tn(a, b):
    return lax.dot_general(a, b, (((0,), (0,)), ((), ())), preferred_element_type=F32)


def dense_body(per_place, place, count, rows, cols, tiles, keep, give_low, give_high):
    tile = tiles.shape[1]
    for out in (keep, give_low, give_high):
        out[...] = jnp.zeros_like(out)
    cut = give_low.shape[1] // tile
    live = count[0, 0]
    batch = 4 if tiles.shape[0] % 4 == 0 else 1

    def put(n, carry):
        turned = [tiles[n * batch + i].T for i in range(batch)]
        for i in range(batch):
            t = n * batch + i
            row = rows[0, 0, t]
            other = (row // per_place) ^ place[0]
            spot = (other // 2) * per_place + row % per_place
            down = pl.ds(pl.multiple_of(cols[0, 0, t] * tile, tile), tile)

            @pl.when((t < live) & (other % 2 == 0))
            def _():
                keep[down, pl.ds(pl.multiple_of(spot * tile, tile), tile)] = turned[i]

            @pl.when((t < live) & (other % 2 == 1) & (spot < cut))
            def _():
                give_low[down, pl.ds(pl.multiple_of(spot * tile, tile), tile)] = turned[i]

            @pl.when((t < live) & (other % 2 == 1) & (spot >= cut))
            def _():
                give_high[down, pl.ds(pl.multiple_of((spot - cut) * tile, tile), tile)] = turned[i]

        return carry

    lax.fori_loop(0, (live + batch - 1) // batch, put, 0)


def product_body(far_size, row, *refs):
    blocks, chunks, outs = refs[:6], refs[6 : 6 + far_size], refs[6 + far_size :]
    deep = outs[0].shape[0] // 2
    length = chunks[0].shape[0]
    for m, out in enumerate(outs):
        at = pl.ds(pl.multiple_of((row[0] ^ (m // 2)) * deep, deep), deep)
        for side in range(2):
            total = 0.0
            for j, chunk in enumerate(chunks):
                if m % 2 == 0:
                    block, n = blocks[side], j
                else:
                    block, n = blocks[2 + 2 * side + j // (far_size // 2)], j % (far_size // 2)
                total = total + mm(block[at, n * length : (n + 1) * length], chunk[...])
            out[side * deep : (side + 1) * deep] = total.astype(BF16)


def grad_body(pre_own, pre_other, mine, theirs, near, far, out):
    deep = pre_own.shape[0]
    for at, pre, turned in ((0, pre_own, deep), (deep, pre_other, 0)):
        hidden = mm_nt(mine[at : at + deep], near[...]) + mm_nt(theirs[turned : turned + deep], far[...])
        out[at : at + deep] = jnp.where(pre[...] > 0, hidden, 0.0).astype(BF16)


def solution(mesh):
    n_row, n_col = mesh.shape["row"], mesh.shape["col"]
    far_size = n_col // 4
    group_size = 2 * n_row

    def permute(value, row_mask, col_mask, name):
        pairs = []
        for r in range(n_row):
            for c in range(n_col):
                pairs.append((r * n_col + c, (r ^ row_mask) * n_col + (c ^ col_mask)))
        with jax.named_scope(name):
            return lax.ppermute(value, ("row", "col"), pairs)

    def to_member(value, m, name):
        return permute(value, m // 2, (m % 2) * 2, f"{name}_{m}")

    def scatter(pieces, name):
        running = pieces[0].astype(F32)
        for m in range(1, group_size):
            running = running + to_member(pieces[m], m, f"{name}_scatter").astype(F32)
        return running

    def along_line(running, name):
        sent = running.astype(BF16)
        for m in range(1, far_size):
            running = running + permute(sent, 0, 4 * m, f"{name}_line_{m}").astype(F32)
        return running.astype(BF16)

    def collect(done, name, ordered=lambda x: x):
        mine = ordered(jnp.stack([done] + [to_member(done, m, f"{name}_gather") for m in range(1, group_size)]))
        return mine, permute(mine, 0, 1, f"{name}_core")

    def shards(adj_tiles, tile_row, tile_col, tile_count, node_feats, pre_act, out_grad, second_weight):
        tiles = adj_tiles[0, 0]
        tile = tiles.shape[1]
        depth, feats = out_grad.shape
        hidden = second_weight.shape[0]
        half = feats // 2
        row_index = lax.axis_index("row").astype(jnp.int32)
        col_index = lax.axis_index("col").astype(jnp.int32)
        core = col_index % 2
        place = col_index // 2
        group = row_index * 2 + place % 2
        span = pre_act.shape[0] * n_row
        rows = depth * n_col
        per_place = 2 * depth // tile

        keep_a, *give_a = local_kernel(
            functools.partial(dense_body, per_place),
            [place.reshape(1), tile_count, tile_row, tile_col],
            [tiles],
            [((span, rows // 2), BF16)] + [((span, rows // 4), BF16)] * 2,
            0,
        )
        both = jnp.stack(after([out_grad, node_feats], keep_a))
        keep = lax.dynamic_slice_in_dim(both, core * half, half, 2)
        give = lax.dynamic_slice_in_dim(both, (1 - core) * half, half, 2)
        got = permute(give, 0, 1, "half_core")
        def lay(i):
            return jnp.concatenate(
                [jnp.where(core == 0, keep[i], got[i]), jnp.where(core == 0, got[i], keep[i])], axis=0
            )

        cot_line, feat_line = {0: lay(0)}, {0: lay(1)}
        near_a = [permute(x, 0, 2, f"block_near_{n}") for n, x in enumerate(give_a)]
        pre_other = permute(after(pre_act, keep_a), 0, 1, "act_core")
        step = far_size // 2
        while step:
            for m in sorted(cot_line):
                cot_line[m + step] = permute(cot_line[m], 0, 4 * step, f"cot_far_{m + step}")
                feat_line[m + step] = permute(
                    after(feat_line[m], cot_line[m + step]), 0, 4 * step, f"feat_far_{m + step}"
                )
            step //= 2
        order = sorted(cot_line)
        late = [after(near_a[0], cot_line[far_size // 2]), after(near_a[1], [cot_line[m] for m in order] + [feat_line[m] for m in order[:-1]])]
        blocks = [keep_a, permute(keep_a, 0, 1, "keep_core")] + near_a
        blocks += [permute(x, 0, 1, f"near_core_{n}") for n, x in enumerate(late)]
        deep = pre_act.shape[0]
        work = 2 * 2 * span * rows * half

        def group_sum(lines, name):
            pieces = local_kernel(
                functools.partial(product_body, far_size),
                [row_index.reshape(1)],
                blocks + [lines[m] for m in order],
                [((2 * deep, half), BF16)] * group_size,
                work,
                8 * 4 * deep * half,
            )
            return scatter(pieces, name).astype(BF16)

        back = group_sum(cot_line, "cot")
        back_far = permute(back, 0, 1, "back_core")
        weight_near = lax.dynamic_slice_in_dim(second_weight, core * half, half, 1)
        weight_far = lax.dynamic_slice_in_dim(second_weight, (1 - core) * half, half, 1)
        (pre_grad,) = local_kernel(
            grad_body,
            [],
            [pre_act, pre_other, back, back_far, weight_near, weight_far],
            [((2 * deep, hidden), BF16)],
            2 * 2 * deep * feats * hidden,
            4 * 4 * deep * hidden,
        )
        feat = group_sum(feat_line, "feat")

        def cut(result, member, outs):
            piece = result.shape[0] // group_size
            for p in range(group_size):
                for m in range(group_size):
                    @pl.when((member[0] ^ m) == p)
                    def _():
                        outs[m][...] = result[p * piece : (p + 1) * piece]

        def second_body(member, pre_a, pre_b, back_ref, *outs):
            result = mm_tn(jnp.maximum(pre_a[...], 0), back_ref[:deep])
            result = result + mm_tn(jnp.maximum(pre_b[...], 0), back_ref[deep:])
            cut(result.astype(BF16), member, outs)

        second_pieces = local_kernel(
            second_body,
            [group.reshape(1)],
            [pre_act, pre_other, back],
            [((hidden // group_size, half), BF16)] * group_size,
            2 * 2 * deep * hidden * half,
            4 * 4 * hidden * half + 4 * deep * hidden,
        )

        def first_body(member, feat_ref, grad_ref, *outs):
            cut(mm_tn(feat_ref[...], grad_ref[...]).astype(BF16), member, outs)

        first_pieces = local_kernel(
            first_body,
            [group.reshape(1)],
            [feat, pre_grad],
            [((half // group_size, hidden), BF16)] * group_size,
            2 * 2 * deep * half * hidden,
            4 * 4 * half * hidden,
        )

        low, high = half // group_size, hidden // group_size

        def by_member(x):
            shape, bit = x.shape, 1
            while bit < group_size:
                y = x.reshape((group_size // (2 * bit), 2, bit) + shape[1:])
                x = jnp.where((group // bit) % 2 == 1, y[:, ::-1], y).reshape(shape)
                bit *= 2
            return x

        where = jnp.stack([group, core])
        second_run = scatter(second_pieces, "second")
        second_done = along_line(after(second_run, first_pieces), "second")
        first_run = scatter(first_pieces, "first")
        mine, theirs = collect(second_done, "second", by_member)
        mine, theirs = mine.reshape(hidden, half), theirs.reshape(hidden, half)
        left, right = jnp.where(core == 0, mine, theirs), jnp.where(core == 0, theirs, mine)
        second = jnp.concatenate([left, right], axis=1).astype(F32)
        first_done = along_line(first_run, "first")
        mine, theirs = collect(first_done, "first", by_member)
        mine, theirs = mine.reshape(half, hidden), theirs.reshape(half, hidden)
        upper, lower = jnp.where(core == 0, mine, theirs), jnp.where(core == 0, theirs, mine)
        first = jnp.concatenate([upper, lower], axis=0).astype(F32)
        return first, second

    in_specs = (
        P("row", "col", None, None, None),
        P("row", "col", None),
        P("row", "col", None),
        P("row", "col"),
        P(("row", "col"), None),
        P(("col", "row"), None),
        P(("row", "col"), None),
        P(),
    )
    out_specs = (P(), P())
    return jax.shard_map(shards, mesh=mesh, in_specs=in_specs, out_specs=out_specs, check_vma=False)
```
